512 devices in a mesh: dp: 8 (over z), expert: 64 (over x, y, core).
Axes of the slice: x: 4, y: 8, z: 8, core: 2. Of those that a mesh axis runs over, the one named last changes fastest.
Arguments:
- cotangent: bfloat16 [65536, 4096], P(('dp', 'expert')), may hold values from -6 to 6
- route_weight: float32 [65536, 8], P(('dp', 'expert')), may hold values from 0.05 to 1
- expert_ids: int32 [65536, 8], P(('dp', 'expert')), may hold values from 0 to 63, as said below
- slot_ids: int32 [65536, 8], P(('dp', 'expert')), may hold values from 0 to 19, as said below
- hidden_saved: bfloat16 [8, 64, 1024, 768], P('dp', 'expert'), may hold values from -6 to 6
- down_weight: bfloat16 [64, 768, 4096], P('expert', None, 'dp'), may hold values from -0.09375 to 0.09375
- adapter_a: bfloat16 [64, 16, 768], P('expert'), may hold values from -0.21875 to 0.21875
- adapter_out_maps: bfloat16 [64, 16, 4096], P('expert'), may hold values from -1.5 to 1.5
- rollout_owner: int32 [64], replicated, may hold values from 0 to 63, each once
Outputs:
- grad_hidden: bfloat16 [8, 64, 1024, 768], P('dp', 'expert')
- grad_a_rollout: bfloat16 [64, 16, 768], P('expert', None, 'dp')
- grad_b_rollout: bfloat16 [64, 16, 4096], P('expert', None, 'dp')
The draws below stay inside these ranges and needn't reach their ends.
Inputs may be any that keep to these rules, and one draw needn't show every extreme that they name: `expert_ids`: the 8 experts of a row are distinct. In each aligned block of 128 rows every expert is named by at most 20 rows, and some expert by exactly that many. `slot_ids`: within an aligned block of 128 rows, the rows that name one expert carry distinct slots, each below the number of such rows; a slot of 16 or more marks a pair beyond capacity.
All inputs are finite; a program needn't handle non-finite values.
Results may differ from the reference program's by a relative error of at most 0.0057.
Values may be sent and summed in bfloat16 or wider, within the bound.
No kernel may reach another device: no remote copies, remote signals or barrier semaphores. Data moves between devices by JAX's collectives and lax.ppermute only.
A program may use at most 128 MiB of HBM per device.

```python
import math
import jax
import jax.numpy as jnp
from jax import lax

D = 4096
FF = 768
RANK = 16
TOP = 8
TOK_DEV = 128
EXPERTS = 64
TOKENS = 65536
CAP = 16
N_DP = 8
N_EXPERT = 64


def routing(key):
    blocks = TOKENS // TOK_DEV
    mean_load = TOK_DEV * TOP // EXPERTS
    step_load = mean_load // 4
    quarter = EXPERTS // 4
    pattern = jnp.concatenate([jnp.full((quarter,), mean_load + step_load, jnp.int32), jnp.full((quarter,), mean_load - step_load, jnp.int32), jnp.full((EXPERTS - 2 * quarter,), mean_load, jnp.int32)])

    def one_block(block):
        first, second = jax.random.split(jax.random.fold_in(key, block))
        counts = pattern[jax.random.permutation(first, EXPERTS)]
        ends = jnp.cumsum(counts).astype(jnp.int32)
        starts = ends - counts
        position = jnp.arange(TOK_DEV * TOP, dtype=jnp.int32)
        expert_number = jnp.searchsorted(ends, position, side='right').astype(jnp.int32)
        slot = position - starts[expert_number]
        order = jax.random.permutation(second, TOK_DEV).astype(jnp.int32)
        row = order[position % TOK_DEV]
        column = position // TOK_DEV
        ids = jnp.zeros((TOK_DEV, TOP), jnp.int32).at[row, column].set(expert_number)
        seats = jnp.zeros((TOK_DEV, TOP), jnp.int32).at[row, column].set(slot)
        return (ids, seats)
    ids, seats = jax.vmap(one_block)(jnp.arange(blocks, dtype=jnp.int32))
    return (ids.reshape(TOKENS, TOP), seats.reshape(TOKENS, TOP))


def draw_expert_ids(key, part):
    ids, seats = routing(key)
    return ids


def draw_slot_ids(key, part):
    ids, seats = routing(key)
    return seats


def level_of(stream_key, extent, shards, low, top_value):
    loudness, own = 1.0, jax.random.fold_in(stream_key, 6)
    for dim, blocks in shards:
        steps = jnp.exp(jax.random.uniform(jax.random.fold_in(own, dim), (blocks,), jnp.float32, low / len(shards), top_value / len(shards)))
        loudness = loudness * jnp.repeat(steps, extent[dim] // blocks).reshape([-1 if axis == dim else 1 for axis in range(len(extent))])
    return loudness


def scatter_about(key, dims, width, bound, cuts=(), kind=jnp.bfloat16):
    array = width * jax.random.normal(key, dims, jnp.float32)
    if cuts:
        array = array * level_of(key, dims, cuts, -0.22, 0.18)
    return jnp.clip(array, -bound, bound).astype(kind)


def setup_inputs(seed: int = 0) -> dict:
    key_of = jax.random.split(jax.random.key(seed), 10)
    return {
        "cotangent": scatter_about(key_of[0], (TOKENS, D), 1.0, 6.0, ((0, 512),)),
        "route_weight": jnp.clip(jnp.exp(math.log(1.0) - 2.9957323 * jax.random.uniform(key_of[1], (TOKENS, TOP), jnp.float32) ** level_of(key_of[1], (TOKENS, TOP), ((0, 512),), -0.2, 0.2)), 0.05, 1.0),
        "expert_ids": draw_expert_ids(jax.random.fold_in(key_of[9], 71), 0),
        "slot_ids": draw_slot_ids(jax.random.fold_in(key_of[9], 71), 0),
        "hidden_saved": scatter_about(key_of[4], (N_DP, EXPERTS, N_EXPERT * CAP, FF), 1.0, 6.0, ((0, 8), (1, 64))),
        "down_weight": scatter_about(key_of[5], (EXPERTS, FF, D), D ** -0.5, 0.09375, ((0, 64), (2, 8))),
        "adapter_a": scatter_about(key_of[6], (EXPERTS, RANK, FF), FF ** -0.5, 0.21875, ((0, 64),)),
        "adapter_out_maps": scatter_about(key_of[7], (EXPERTS, RANK, D), RANK ** -0.5, 1.5, ((0, 64),)),
        "rollout_owner": jax.random.permutation(key_of[8], EXPERTS).astype(jnp.int32),
    }


ADAPTER_SCALE = 2.0


def reference(cotangent, route_weight, expert_ids, slot_ids, hidden_saved, down_weight, adapter_a, adapter_out_maps, rollout_owner):
    group_rows = TOK_DEV * N_EXPERT
    slots_per = N_EXPERT * CAP

    def one_group(carry, group):
        start = (group * group_rows).astype(jnp.int32)
        rows = lax.dynamic_slice_in_dim(cotangent, start, group_rows, 0)
        weights = lax.dynamic_slice_in_dim(route_weight, start, group_rows, 0).reshape(-1)
        ids = lax.dynamic_slice_in_dim(expert_ids, start, group_rows, 0)
        slots = lax.dynamic_slice_in_dim(slot_ids, start, group_rows, 0)
        source = jnp.arange(group_rows, dtype=jnp.int32) // TOK_DEV
        keep = slots < CAP
        flat_pos = jnp.where(keep, ids * slots_per + source[:, None] * CAP + slots, EXPERTS * slots_per).reshape(-1).astype(jnp.int32)
        anchor = jnp.zeros((EXPERTS * slots_per,), jnp.int32).at[flat_pos].set(jnp.arange(group_rows * TOP, dtype=jnp.int32), mode="drop")
        filled = jnp.zeros((EXPERTS * slots_per,), jnp.float32).at[flat_pos].set(1.0, mode="drop")
        hidden_group = lax.dynamic_index_in_dim(hidden_saved, group.astype(jnp.int32), 0, keepdims=False)

        def per_expert(expert_number):
            base = (expert_number * slots_per).astype(jnp.int32)
            src = lax.dynamic_slice_in_dim(anchor, base, slots_per, 0)
            live = lax.dynamic_slice_in_dim(filled, base, slots_per, 0)
            routed_tokens = (weights[src][:, None] * rows[src // TOP].astype(jnp.float32) * live[:, None]).astype(jnp.bfloat16)
            hidden = hidden_group[expert_number]
            rank_feature_block = (ADAPTER_SCALE * jnp.dot(routed_tokens, adapter_out_maps[expert_number].T, preferred_element_type=jnp.float32)).astype(jnp.bfloat16)
            hidden_projection = jnp.dot(hidden, adapter_a[expert_number].T, preferred_element_type=jnp.float32).astype(jnp.bfloat16)
            back = jnp.dot(routed_tokens, down_weight[expert_number].T, preferred_element_type=jnp.float32)
            back = (back + jnp.dot(rank_feature_block, adapter_a[expert_number], preferred_element_type=jnp.float32)).astype(jnp.bfloat16)
            out_map_gradient = ADAPTER_SCALE * jnp.dot(hidden_projection.T, routed_tokens, preferred_element_type=jnp.float32)
            grad_a = jnp.dot(rank_feature_block.T, hidden, preferred_element_type=jnp.float32)
            return grad_a, out_map_gradient, back

        grad_a, out_map_gradient, back = lax.map(per_expert, jnp.arange(EXPERTS, dtype=jnp.int32))
        return (carry[0] + grad_a, carry[1] + out_map_gradient), back

    init = (jnp.zeros((EXPERTS, RANK, FF), jnp.float32), jnp.zeros((EXPERTS, RANK, D), jnp.float32))
    (sum_a, sum_b), grad_hidden = lax.scan(one_group, init, jnp.arange(N_DP, dtype=jnp.int32))
    out_a = jnp.zeros((EXPERTS, RANK, FF), jnp.bfloat16).at[rollout_owner].set(sum_a.astype(jnp.bfloat16))
    out_b = jnp.zeros((EXPERTS, RANK, D), jnp.bfloat16).at[rollout_owner].set(sum_b.astype(jnp.bfloat16))
    return grad_hidden, out_a, out_b
```

```python
import functools

import jax
import jax.numpy as jnp
from jax import lax
from jax.experimental import pallas as pl
from jax.experimental.pallas import tpu as pltpu
from jax.sharding import Mesh, PartitionSpec as P

ADAPTER_SCALE = 2.0
GROUPS, NX, NY, NC = 8, 4, 8, 2
COLS = NX * NC
CAP = 16
META = 128
MIB = 1024 * 1024
VM = pl.BlockSpec(memory_space=pltpu.VMEM)
SM = pl.BlockSpec(memory_space=pltpu.SMEM)
NT = (((1,), (1,)), ((), ()))
TN = (((0,), (0,)), ((), ()))
NN = (((1,), (0,)), ((), ()))


def dot(a, b, dims):
    return lax.dot_general(a, b, dims, preferred_element_type=jnp.float32)


def params(mib):
    return pltpu.CompilerParams(vmem_limit_bytes=mib * MIB)


def pack_kernel(cot, weight, ids, slots, out):
    width = cot.shape[1]
    out[:, :width] = cot[...]
    w = weight[...]
    hi = w.astype(jnp.bfloat16)
    rest = w - hi.astype(jnp.float32)
    mid = rest.astype(jnp.bfloat16)
    low = (rest - mid.astype(jnp.float32)).astype(jnp.bfloat16)
    zero = jnp.zeros(low.shape, jnp.float32)
    rows = [
        ids[...].astype(jnp.float32),
        slots[...].astype(jnp.float32),
        hi.astype(jnp.float32),
        mid.astype(jnp.float32),
        low.astype(jnp.float32),
        zero,
    ]
    table = jnp.concatenate(rows, axis=0).astype(jnp.bfloat16)
    out[0:48, width:] = table
    out[48:, width:] = jnp.zeros((out.shape[0] - 48, META), jnp.bfloat16)


def pack(cot, weight, ids, slots):
    return pl.pallas_call(
        pack_kernel,
        out_shape=jax.ShapeDtypeStruct((cot.shape[0], cot.shape[1] + META), jnp.bfloat16),
        in_specs=[VM] * 4,
        out_specs=VM,
        compiler_params=params(12),
    )(cot, weight, ids, slots)


def build_kernel(halves, me, *refs):
    out = refs[-1]
    blocks = refs[:-1]
    count = 1 if halves else len(blocks)
    for b in range(count):
        first = blocks[b]
        width = first.shape[1] - META
        table = first[0:48, width:].astype(jnp.float32)
        expert = table[0:8].astype(jnp.int32)
        slot = table[8:16].astype(jnp.int32)
        weight = table[16:24] + table[24:32] + table[32:40]
        dest = (expert // (NY * NC)) * NC + expert % NC
        here = ((expert // NC) % NY == me[0]) & (slot < CAP)
        code = jnp.where(here, dest * CAP + slot, -1)
        tokens = code.shape[1]
        row = lax.broadcasted_iota(jnp.int32, (COLS * CAP, tokens), 0)
        pick = jnp.zeros((COLS * CAP, tokens), jnp.float32)
        scale = jnp.zeros((COLS * CAP, tokens), jnp.float32)
        for k in range(code.shape[0]):
            match = row == code[k : k + 1]
            pick = jnp.where(match, 1.0, pick)
            scale = jnp.where(match, weight[k : k + 1], scale)
        scale = jnp.sum(scale, axis=1, keepdims=True)
        pick = pick.astype(jnp.bfloat16)
        step = 1024
        for at in range(0, width, step):
            if halves:
                value = jnp.concatenate([blocks[0][:, at : at + step], blocks[1][:, at : at + step]], axis=0)
            else:
                value = first[:, at : at + step]
            rows = (scale * dot(pick, value, NN)).astype(jnp.bfloat16)
            out[:, b, :, at : at + step] = rows.reshape(COLS, CAP, step)


def build(me, blocks, halves=False):
    width = blocks[0].shape[1] - META
    count = 1 if halves else len(blocks)
    return pl.pallas_call(
        functools.partial(build_kernel, halves),
        out_shape=jax.ShapeDtypeStruct((COLS, count, CAP, width), jnp.bfloat16),
        in_specs=[SM] + [VM] * len(blocks),
        out_specs=VM,
        compiler_params=params(20),
    )(me, *blocks)


def places(me, offsets):
    found = []
    for x in range(NX):
        for c in range(NC):
            for offset in offsets:
                found.append(x * NY * NC + ((me + offset + NY) % NY) * NC + c)
    return found


def grads_kernel(offsets, first, last, *refs):
    if first:
        me, g, hidden, amap, bmap = refs[:5]
        old_a = old_b = None
        rest = refs[5:]
    else:
        me, g, hidden, amap, bmap, old_a, old_b = refs[:7]
        rest = refs[7:]
    hid = rest[-1]
    outs = rest[:-1]
    for i, src in enumerate(places(me[0], offsets)):
        hid[i * CAP : (i + 1) * CAP] = hidden[src]
    rows = hid.shape[0]
    width = g.shape[-1]
    tokens = g[...].reshape(rows, width)
    rb = (ADAPTER_SCALE * dot(tokens, bmap[...], NT)).astype(jnp.bfloat16)
    outs[0][...] = rb
    z = dot(hid[...], amap[...], NT).astype(jnp.bfloat16)
    grad_b = ADAPTER_SCALE * dot(z, tokens, TN)
    grad_a = dot(rb, hid[...], TN)
    if old_a is not None:
        grad_b = grad_b + old_b[...]
        grad_a = grad_a + old_a[...]
    if not last:
        outs[1][...] = grad_a
        outs[2][...] = grad_b
    else:
        sent = outs[1]
        wide_b = width // GROUPS
        wide_a = hid.shape[1] // GROUPS
        for z_to in range(GROUPS):
            sent[z_to, :, :wide_b] = grad_b[:, z_to * wide_b : (z_to + 1) * wide_b].astype(jnp.bfloat16)
            sent[z_to, :, wide_b : wide_b + wide_a] = grad_a[:, z_to * wide_a : (z_to + 1) * wide_a].astype(
                jnp.bfloat16
            )


def grads(me, g, hidden, amap, bmap, old, offsets, last):
    rows = g.shape[0] * g.shape[1] * g.shape[2]
    rank, width = bmap.shape
    hidden_width = amap.shape[1]
    shapes = [jax.ShapeDtypeStruct((rows, rank), jnp.bfloat16)]
    if last:
        piece = width // GROUPS + hidden_width // GROUPS
        shapes += [jax.ShapeDtypeStruct((GROUPS, rank, piece), jnp.bfloat16)]
    else:
        shapes += [
            jax.ShapeDtypeStruct((rank, hidden_width), jnp.float32),
            jax.ShapeDtypeStruct((rank, width), jnp.float32),
        ]
    args = [me, g, hidden, amap, bmap] + list(old)
    return pl.pallas_call(
        functools.partial(grads_kernel, offsets, not old, last),
        out_shape=shapes,
        in_specs=[SM] + [VM] * (len(args) - 1),
        out_specs=[VM] * len(shapes),
        scratch_shapes=[pltpu.VMEM((rows, hidden_width), jnp.bfloat16)],
        compiler_params=params(20),
    )(*args)


def back_kernel(chunks, me, weight, amap, *refs):
    out = refs[-1]
    for n, offsets in enumerate(chunks):
        g, rb = refs[2 * n], refs[2 * n + 1]
        rows = rb.shape[0]
        width = g.shape[-1]
        wide = weight.shape[-1]
        total = dot(rb[...], amap[...], NN)
        for z in range(GROUPS):
            total = total + dot(g[:, :, :, z * wide : (z + 1) * wide].reshape(rows, wide), weight[z], NT)
        total = total.astype(jnp.bfloat16)
        for i, src in enumerate(places(me[0], offsets)):
            out[src] = total[i * CAP : (i + 1) * CAP]


def back(me, weight, amap, pairs, chunks):
    flat = [ref for pair in pairs for ref in pair]
    return pl.pallas_call(
        functools.partial(back_kernel, chunks),
        out_shape=jax.ShapeDtypeStruct((NX * NY * NC, CAP, amap.shape[1]), jnp.bfloat16),
        in_specs=[SM] + [VM] * (2 + len(flat)),
        out_specs=VM,
        compiler_params=params(32),
    )(me, weight, amap, *flat)


def spread_kernel(got, out):
    total = jnp.sum(got[...].astype(jnp.float32), axis=0).astype(jnp.bfloat16)
    for d in range(COLS):
        out[d] = total


def spread(got):
    return pl.pallas_call(
        spread_kernel,
        out_shape=jax.ShapeDtypeStruct((COLS,) + got.shape[1:], got.dtype),
        in_specs=[VM],
        out_specs=VM,
    )(got)


def turn_kernel(where, owner, got, out):
    x, y, c = where[0], where[1], where[2]
    for y_to in range(NY):
        target = x * NY * NC + y_to * NC + c
        for s in range(COLS):
            expert = (s // NC) * NY * NC + y * NC + s % NC

            @pl.when(owner[expert] == target)
            def _():
                out[y_to] = got[s]


def turn(where, owner, got):
    return pl.pallas_call(
        turn_kernel,
        out_shape=jax.ShapeDtypeStruct((NY,) + got.shape[1:], got.dtype),
        in_specs=[SM, SM, VM],
        out_specs=VM,
    )(where, owner, got)


def take_kernel(wide_b, where, owner, got, out_a, out_b):
    mine = (where[0] * NY + where[1]) * NC + where[2]
    for expert in range(NX * NY * NC):

        @pl.when(owner[expert] == mine)
        def _():
            row = got[(expert // NC) % NY]
            out_b[...] = row[:, :wide_b]
            out_a[...] = row[:, wide_b:]


def take(where, owner, got, wide_a, wide_b):
    rank = got.shape[1]
    return pl.pallas_call(
        functools.partial(take_kernel, wide_b),
        out_shape=[
            jax.ShapeDtypeStruct((rank, wide_a), got.dtype),
            jax.ShapeDtypeStruct((rank, wide_b), got.dtype),
        ],
        in_specs=[SM, SM, VM],
        out_specs=[VM, VM],
    )(where, owner, got)


def per_device(
    cotangent,
    route_weight,
    expert_ids,
    slot_ids,
    hidden_saved,
    down_weight,
    adapter_a,
    adapter_out_maps,
    rollout_owner,
):
    width = cotangent.shape[1]
    hidden_width = adapter_a.shape[2]
    x = lax.axis_index("x").astype(jnp.int32)
    y = lax.axis_index("y").astype(jnp.int32)
    c = lax.axis_index("core").astype(jnp.int32)
    me = y.reshape(1)
    where = jnp.stack([x, y, c])
    up = [(i, (i + 1) % NY) for i in range(NY)]
    down = [(i, (i - 1) % NY) for i in range(NY)]
    row = ("x", "core")

    weight = lax.all_gather(down_weight[0], "dp")
    own = pack(cotangent, route_weight.T, expert_ids.T, slot_ids.T)
    hidden = hidden_saved.reshape(NX * NY * NC, CAP, hidden_width)
    amap = adapter_a[0]
    bmap = adapter_out_maps[0]

    def send(rows):
        return lax.all_to_all(rows, row, 0, 0, tiled=True)

    chunks = [(0,)] + [(-d, d) for d in range(1, NY // 2)] + [(NY // 2,)]
    from_down, from_up = own, own
    arrived = [send(build(me, [own]))]
    for d in range(1, NY // 2):
        from_down = lax.ppermute(from_down, "y", up)
        from_up = lax.ppermute(from_up, "y", down)
        arrived.append(send(build(me, [from_down, from_up])))
    half = own.shape[0] // 2
    far_low = lax.ppermute(from_down[:half], "y", up)
    far_high = lax.ppermute(from_up[half:], "y", down)
    arrived.append(send(build(me, [far_low, far_high], halves=True)))

    old = ()
    pairs = []
    for n, offsets in enumerate(chunks):
        last = n == len(chunks) - 1
        rb, *old = grads(me, arrived[n], hidden, amap, bmap, old, offsets, last)
        pairs.append((arrived[n], rb))
    sent = old[0]
    got = lax.all_to_all(sent, "dp", 0, 0, tiled=True)
    row_items = lax.all_to_all(spread(got), row, 0, 0, tiled=True)
    column_items = lax.all_to_all(turn(where, rollout_owner, row_items), "y", 0, 0, tiled=True)
    out_a, out_b = take(where, rollout_owner, column_items, hidden_width // GROUPS, width // GROUPS)
    grad_hidden = back(me, weight, amap, pairs, chunks)
    return (
        grad_hidden.reshape(1, 1, NX * NY * NC * CAP, hidden_width),
        out_a[None],
        out_b[None],
    )


def solution(mesh):
    parts = Mesh(mesh.devices.reshape(GROUPS, NX, NY, NC), ("dp", "x", "y", "core"))
    every = ("dp", "x", "y", "core")
    expert = ("x", "y", "core")
    return jax.shard_map(
        per_device,
        mesh=parts,
        in_specs=(
            P(every, None),
            P(every, None),
            P(every, None),
            P(every, None),
            P("dp", expert, None, None),
            P(expert, None, "dp"),
            P(expert, None, None),
            P(expert, None, None),
            P(),
        ),
        out_specs=(P("dp", expert, None, None), P(expert, None, "dp"), P(expert, None, "dp")),
        check_vma=False,
    )
```

```python
import functools

import jax
import jax.numpy as jnp
from jax import lax
from jax.experimental import pallas as pl
from jax.experimental.pallas import tpu as pltpu
from jax.sharding import Mesh, PartitionSpec as P

ADAPTER_SCALE = 2.0
COST_BUILD, COST_GRADS, COST_BACK = 8, 3, 10
GROUPS, NX, NY, NC = 8, 4, 8, 2
COLS = NX * NC
CAP = 16
META = 128
MIB = 1024 * 1024
VM = pl.BlockSpec(memory_space=pltpu.VMEM)
ANY = pl.BlockSpec(memory_space=pl.ANY)
HBM = pl.BlockSpec(memory_space=pltpu.HBM)
SM = pl.BlockSpec(memory_space=pltpu.SMEM)
NT = (((1,), (1,)), ((), ()))
TN = (((0,), (0,)), ((), ()))
NN = (((1,), (0,)), ((), ()))


def dot(a, b, dims):
    return lax.dot_general(a, b, dims, preferred_element_type=jnp.float32)


def params(mib):
    return pltpu.CompilerParams(vmem_limit_bytes=mib * MIB)


def cost(us):
    return pl.CostEstimate(flops=int(us * 1.0e9), bytes_accessed=int(us * 3.0e6), transcendentals=0)


def copies(pairs, sems):
    started = [pltpu.make_async_copy(src, dst, sems.at[i]) for i, (src, dst) in enumerate(pairs)]
    for copy in started:
        copy.start()
    return started


def pack_kernel(cot, weight, ids, slots, out, w_in, ids_in, slots_in, sems):
    width = cot.shape[1]
    coming = copies([(weight, w_in), (ids, ids_in), (slots, slots_in), (cot, out.at[:, pl.ds(0, width)])], sems)
    out[48:, width:] = jnp.zeros((out.shape[0] - 48, META), jnp.bfloat16)
    for copy in coming[:3]:
        copy.wait()
    w = w_in[...]
    hi = w.astype(jnp.bfloat16)
    rest = w - hi.astype(jnp.float32)
    mid = rest.astype(jnp.bfloat16)
    low = (rest - mid.astype(jnp.float32)).astype(jnp.bfloat16)
    rows = [
        ids_in[...].astype(jnp.float32),
        slots_in[...].astype(jnp.float32),
        hi.astype(jnp.float32),
        mid.astype(jnp.float32),
        low.astype(jnp.float32),
        jnp.zeros(low.shape, jnp.float32),
    ]
    out[0:48, width:] = jnp.concatenate(rows, axis=0).astype(jnp.bfloat16)
    coming[3].wait()


def pack(cot, weight, ids, slots):
    return pl.pallas_call(
        pack_kernel,
        name="pack",
        out_shape=jax.ShapeDtypeStruct((cot.shape[0], cot.shape[1] + META), jnp.bfloat16),
        in_specs=[HBM] * 4,
        out_specs=VM,
        scratch_shapes=[pltpu.VMEM(a.shape, a.dtype) for a in (weight, ids, slots)]
        + [pltpu.SemaphoreType.DMA((4,))],
        compiler_params=params(12),
        cost_estimate=cost(2),
    )(cot, weight, ids, slots)


def gate(values, after):
    return list(lax.optimization_barrier((tuple(values), tuple(after)))[0])


def build_kernel(numbered, me, *refs):
    blocks, (out, made, sems) = refs[:-3], refs[-3:]
    count = made.shape[2]
    for b in range(count):
        block = blocks[b]
        width = block.shape[1] - META
        routes = block[0:48, width:].astype(jnp.float32)
        expert = routes[0:8].astype(jnp.int32)
        slot = routes[8:16].astype(jnp.int32)
        weight = routes[16:24] + routes[24:32] + routes[32:40]
        across = expert % NC if numbered else (expert % NC + me[2]) % NC
        here = ((expert // NC) % NY == me[1]) & (slot < CAP)
        code = jnp.where(here, (expert // (NY * NC) * NC + across) * CAP + slot, -1)
        row = lax.broadcasted_iota(jnp.int32, (COLS * CAP, code.shape[1]), 0)
        pick = jnp.zeros(row.shape, jnp.float32)
        scale = jnp.zeros(row.shape, jnp.float32)
        for k in range(code.shape[0]):
            match = row == code[k : k + 1]
            pick = jnp.where(match, 1.0, pick)
            scale = jnp.where(match, weight[k : k + 1], scale)
        scale = jnp.sum(scale, axis=1, keepdims=True)
        pick = pick.astype(jnp.bfloat16)
        step = 1024
        for at in range(0, width, step):
            rows = (scale * dot(pick, block[:, at : at + step], NN)).astype(jnp.bfloat16)
            for d in range(COLS):
                made[d // NC, d % NC, b, :, at : at + step] = rows[d * CAP : (d + 1) * CAP]
    for copy in copies([(made.at[x], out.at[x]) for x in range(NX)], sems):
        copy.wait()


def build(n, me, blocks, numbered=False):
    width = blocks[0].shape[1] - META
    shape = (NX, NC, len(blocks), CAP, width)
    return pl.pallas_call(
        functools.partial(build_kernel, numbered),
        name=f"build_{n}",
        out_shape=jax.ShapeDtypeStruct(shape, jnp.bfloat16),
        in_specs=[SM] + [VM] * len(blocks),
        out_specs=HBM,
        scratch_shapes=[pltpu.VMEM(shape, jnp.bfloat16), pltpu.SemaphoreType.DMA((NX,))],
        compiler_params=params(8),
        cost_estimate=cost(COST_BUILD),
    )(me, *blocks)


def places(me, offsets):
    whole = offsets == (NY // 2,)
    order = [(x, c) for x in range(NX) for c in range(NC)]
    if not whole:
        order = [(x, (me[2] + dc) % NC) for dc in range(NC) for x in range(NX)]
    return [(x * NY + (me[1] + offset + NY) % NY) * NC + c for x, c in order for offset in offsets]


def grads_kernel(chunk, count, first, last, waits, *refs):
    me, refs = refs[0], refs[1 + waits :]
    parts, (hidden, amap, bmap), refs = refs[:count], refs[count : count + 3], refs[count + 3 :]
    old_a, old_b = (None, None) if first else refs[:2]
    rest = refs if first else refs[2:]
    hid, tok, sems = rest[-3:]
    outs = rest[:-3]
    if count == 1:
        coming = copies([(parts[0], tok)], sems)
    else:
        coming = copies([(parts[0].at[:, 0], tok.at[pl.ds(0, NX)])], sems)
    for i, src in enumerate(places(me, chunk)):
        hid[i * CAP : (i + 1) * CAP] = hidden[src]
    rows, width = hid.shape[0], tok.shape[-1]
    z = dot(hid[...], amap[...], NT).astype(jnp.bfloat16)
    if count == 2:
        tok[NX:] = parts[1][...]
    for copy in coming:
        copy.wait()
    tokens = tok[...].reshape(rows, width)
    rb = (ADAPTER_SCALE * dot(tokens, bmap[...], NT)).astype(jnp.bfloat16)
    outs[0][...] = rb
    grad_b = ADAPTER_SCALE * dot(z, tokens, TN)
    grad_a = dot(rb, hid[...], TN)
    if old_a is not None:
        grad_b = grad_b + old_b[...]
        grad_a = grad_a + old_a[...]
    if not last:
        outs[1][...] = grad_a
        outs[2][...] = grad_b
    else:
        sent = outs[1]
        wide_b = width // GROUPS
        wide_a = hid.shape[1] // GROUPS
        for z_to in range(GROUPS):
            sent[z_to, :, :wide_b] = grad_b[:, z_to * wide_b : (z_to + 1) * wide_b].astype(jnp.bfloat16)
            sent[z_to, :, wide_b : wide_b + wide_a] = grad_a[:, z_to * wide_a : (z_to + 1) * wide_a].astype(
                jnp.bfloat16
            )


def grads(n, me, parts, hidden, amap, bmap, old, chunk, last, after=()):
    pieces = COLS * len(chunk)
    rows = pieces * CAP
    rank, width = bmap.shape
    hidden_width = amap.shape[1]
    shapes = [jax.ShapeDtypeStruct((rows, rank), jnp.bfloat16)]
    if last:
        piece = width // GROUPS + hidden_width // GROUPS
        shapes += [jax.ShapeDtypeStruct((GROUPS, rank, piece), jnp.bfloat16)]
    else:
        shapes += [
            jax.ShapeDtypeStruct((rank, hidden_width), jnp.float32),
            jax.ShapeDtypeStruct((rank, width), jnp.float32),
        ]
    args = [hidden, amap, bmap] + list(old)
    return pl.pallas_call(
        functools.partial(grads_kernel, chunk, len(parts), not old, last, len(after)),
        name=f"grads_{n}",
        out_shape=shapes,
        in_specs=[SM] + [ANY] * len(after) + [HBM] + [VM] * (len(parts) - 1 + len(args)),
        out_specs=[VM] * len(shapes),
        scratch_shapes=[
            pltpu.VMEM((rows, hidden_width), jnp.bfloat16),
            pltpu.VMEM((COLS, len(chunk), CAP, width), jnp.bfloat16),
            pltpu.SemaphoreType.DMA((1,)),
        ],
        compiler_params=params(10),
        cost_estimate=cost(COST_GRADS),
    )(me, *after, *parts, *args)


def back_kernel(chunks, counts, more, me, weight, *refs):
    count = len(chunks)
    straights, refs = refs[:count], refs[count:]
    crosseds, refs = refs[: sum(counts) - count], refs[sum(counts) - count :]
    rbs, amap, refs = refs[:count], refs[count], refs[count + 1 + more :]
    out, toks, done = refs[0], refs[1 : 1 + count], refs[1 + count : 1 + 2 * count]
    sems, sems_out = refs[-2:]
    pairs = []
    for n in range(count):
        pairs.append((straights[n] if counts[n] == 1 else straights[n].at[:, 0], toks[n]))
    coming = copies(pairs, sems)
    going = []
    for n, chunk in enumerate(chunks):
        wide = weight.shape[-1]
        total = dot(rbs[n][...], amap[...], NN)
        coming[n].wait()
        parts = [toks[n]] + ([crosseds[n]] if counts[n] == 2 else [])
        for z in range(GROUPS):
            g = [part[:, :, :, z * wide : (z + 1) * wide].reshape(-1, wide) for part in parts]
            total = total + dot(jnp.concatenate(g, axis=0), weight[z], NT)
        done[n][...] = total.astype(jnp.bfloat16).reshape(done[n].shape)
        for i, src in enumerate(places(me, chunk)):
            copy = pltpu.make_async_copy(done[n].at[i], out.at[src], sems_out.at[len(going)])
            copy.start()
            going.append(copy)
    for copy in going:
        copy.wait()


def back(n, me, weight, amap, work, chunks, old=()):
    straights = [parts[0] for parts, rb in work]
    crosseds = [parts[1] for parts, rb in work if len(parts) == 2]
    rbs = [rb for parts, rb in work]
    counts = [len(parts) for parts, rb in work]
    hidden_width = amap.shape[1]
    pieces = [rb.shape[0] // CAP for rb in rbs]
    toks = [(COLS // len(parts),) + parts[0].shape[-3:] for parts, rb in work]
    return pl.pallas_call(
        functools.partial(back_kernel, chunks, counts, len(old)),
        name=f"back_{n}",
        out_shape=jax.ShapeDtypeStruct((NX * NY * NC, CAP, hidden_width), jnp.bfloat16),
        in_specs=[SM, VM] + [HBM] * len(work) + [VM] * (len(crosseds) + len(rbs) + 1) + [HBM] * len(old),
        out_specs=HBM,
        input_output_aliases={3 + sum(counts) + len(rbs): 0} if old else {},
        scratch_shapes=[pltpu.VMEM(tok, jnp.bfloat16) for tok in toks]
        + [pltpu.VMEM((piece, CAP, hidden_width), jnp.bfloat16) for piece in pieces]
        + [pltpu.SemaphoreType.DMA((len(work),)), pltpu.SemaphoreType.DMA((sum(pieces),))],
        compiler_params=params(14),
        cost_estimate=cost(COST_BACK),
    )(me, weight, *straights, *crosseds, *rbs, amap, *old)


def spread_kernel(got, out):
    total = jnp.sum(got[...].astype(jnp.float32), axis=0).astype(jnp.bfloat16)
    for d in range(COLS):
        out[d] = total


def spread(got):
    return pl.pallas_call(
        spread_kernel,
        name="spread",
        out_shape=jax.ShapeDtypeStruct((COLS,) + got.shape[1:], got.dtype),
        in_specs=[VM],
        out_specs=VM,
    )(got)


def turn_kernel(where, got, out):
    for y_to in range(NY):
        out[y_to] = got[where[y_to]]


def turn(where, got):
    return pl.pallas_call(
        turn_kernel,
        name="turn",
        out_shape=jax.ShapeDtypeStruct((NY,) + got.shape[1:], got.dtype),
        in_specs=[SM, VM],
        out_specs=VM,
    )(where, got)


def take_kernel(wide_b, where, got, out_a, out_b):
    row = got[where[NY]]
    out_b[...] = row[:, :wide_b]
    out_a[...] = row[:, wide_b:]


def take(where, got, wide_a, wide_b):
    rank = got.shape[1]
    return pl.pallas_call(
        functools.partial(take_kernel, wide_b),
        name="take",
        out_shape=[
            jax.ShapeDtypeStruct((rank, wide_a), got.dtype),
            jax.ShapeDtypeStruct((rank, wide_b), got.dtype),
        ],
        in_specs=[SM, VM],
        out_specs=[VM, VM],
    )(where, got)


def per_device(
    cotangent,
    route_weight,
    expert_ids,
    slot_ids,
    hidden_saved,
    down_weight,
    adapter_a,
    adapter_out_maps,
    rollout_owner,
):
    width = cotangent.shape[1]
    hidden_width = adapter_a.shape[2]
    x = lax.axis_index("x").astype(jnp.int32)
    y = lax.axis_index("y").astype(jnp.int32)
    c = lax.axis_index("core").astype(jnp.int32)
    me = jnp.stack([x, y, c])
    up = [(i, (i + 1) % NY) for i in range(NY)]
    down = [(i, (i - 1) % NY) for i in range(NY)]
    row = ("x", "core")
    experts = jnp.arange(NX * NY * NC, dtype=jnp.int32)
    takers = (x * NY + jnp.append(jnp.arange(NY, dtype=jnp.int32), y)) * NC + c
    taken = jnp.sum(jnp.where(rollout_owner[None, :] == takers[:, None], experts[None, :], 0), axis=1)
    beside = taken // (NY * NC) * NC + taken % NC
    where = jnp.where(jnp.arange(NY + 1) < NY, beside, taken // NC % NY)

    def send(built):
        return lax.all_to_all(built, "x", 0, 0, tiled=True)

    def cross(straight):
        return straight, lax.ppermute(straight[:, 1], "core", [(0, 1), (1, 0)])

    own = pack(cotangent, route_weight.T, expert_ids.T, slot_ids.T)
    weight = lax.all_gather(down_weight[0], "dp")
    hidden = hidden_saved.reshape(NX * NY * NC, CAP, hidden_width)
    amap = adapter_a[0]
    bmap = adapter_out_maps[0]

    chunks = [(0,)] + [(-d, d) for d in range(1, NY // 2)] + [(NY // 2,)]
    last = len(chunks) - 1
    old = ()
    work = []
    whole = []

    def settle(after=()):
        nonlocal old
        n = len(work)
        parts = whole[n]
        rb, *old = grads(n, me, parts, hidden, amap, bmap, old, chunks[n], n == last, after)
        work.append((parts, rb))
        return rb

    either = [(i * NC, (i + 1) % NY * NC) for i in range(NY)] + [(i * NC + 1, (i - 1) % NY * NC + 1) for i in range(NY)]
    held = [own]
    for w in range(1, last + 1):
        low, high = held[0], held[-1]
        if w < last:
            ahead = [lax.ppermute(low, "y", up), lax.ppermute(high, "y", down)]
        else:
            ahead = [lax.ppermute(jnp.where(c == 0, low, high), ("y", "core"), either)]
        done = []
        if w >= 3:
            done.append(settle())
        built = build(w - 1, me, held)
        straight = send(built)
        if w < last:
            whole.append(cross(straight))
        held = [gate([block], done + [built, where])[0] for block in ahead]
    built = build(last, me, held, True)
    final = lax.all_to_all(built.reshape((COLS,) + built.shape[2:]), row, 0, 0, tiled=True)
    rb = settle()
    whole.append(cross(gate([straight], [built, rb])[0]))
    rb = settle()
    whole.append(gate([final], [rb]))
    settle()

    def turn_back(n, begin, end, filled):
        return back(n, me, weight, amap, work[begin:end], chunks[begin:end], filled)

    got = lax.all_to_all(old[0], "dp", 0, 0, tiled=True)
    filled = turn_back(0, 0, 2, [])
    got, filled = gate([got, filled], [])
    row_items = lax.all_to_all(spread(got), row, 0, 0, tiled=True)
    filled = turn_back(1, 2, 3, [filled])
    row_items, filled = gate([row_items, filled], [])
    column_items = lax.all_to_all(turn(where, row_items), "y", 0, 0, tiled=True)
    filled = turn_back(2, 3, 5, [filled])
    column_items, grad_hidden = gate([column_items, filled], [])
    out_a, out_b = take(where, column_items, hidden_width // GROUPS, width // GROUPS)
    return (
        grad_hidden.reshape(1, 1, NX * NY * NC * CAP, hidden_width),
        out_a[None],
        out_b[None],
    )


def solution(mesh):
    parts = Mesh(mesh.devices.reshape(GROUPS, NX, NY, NC), ("dp", "x", "y", "core"))
    every = ("dp", "x", "y", "core")
    expert = ("x", "y", "core")
    return jax.shard_map(
        per_device,
        mesh=parts,
        in_specs=(
            P(every, None),
            P(every, None),
            P(every, None),
            P(every, None),
            P("dp", expert, None, None),
            P(expert, None, "dp"),
            P(expert, None, None),
            P(expert, None, None),
            P(),
        ),
        out_specs=(P("dp", expert, None, None), P(expert, None, "dp"), P(expert, None, "dp")),
        check_vma=False,
    )
```

```python
import functools

import jax
import jax.numpy as jnp
from jax import lax
from jax.experimental import pallas as pl
from jax.experimental.pallas import tpu as pltpu
from jax.sharding import Mesh, PartitionSpec as P

ADAPTER_SCALE = 2.0
COST_BUILD, COST_GRADS, COST_BACK = 8, 3, 10
GROUPS, NX, NY, NC = 8, 4, 8, 2
COLS = NX * NC
CAP = 16
META = 128
WHOLE, CROSS, SPLIT = 0, 1, 2
PARTS = {WHOLE: 1, CROSS: 2, SPLIT: COLS}
MIB = 1024 * 1024
VM = pl.BlockSpec(memory_space=pltpu.VMEM)
ANY = pl.BlockSpec(memory_space=pl.ANY)
HBM = pl.BlockSpec(memory_space=pltpu.HBM)
SM = pl.BlockSpec(memory_space=pltpu.SMEM)
NT = (((1,), (1,)), ((), ()))
TN = (((0,), (0,)), ((), ()))
NN = (((1,), (0,)), ((), ()))


def dot(a, b, dims):
    return lax.dot_general(a, b, dims, preferred_element_type=jnp.float32)


def params(mib):
    return pltpu.CompilerParams(vmem_limit_bytes=mib * MIB)


def cost(us):
    return pl.CostEstimate(flops=int(us * 1.0e9), bytes_accessed=int(us * 3.0e6), transcendentals=0)


def far_memory(array):
    return pltpu.with_memory_space_constraint(array, pltpu.HBM)


def copies(pairs, sems, first=0):
    started = [pltpu.make_async_copy(src, dst, sems.at[first + i]) for i, (src, dst) in enumerate(pairs)]
    for copy in started:
        copy.start()
    return started


def pack_kernel(cot, weight, ids, slots, out, w_in, ids_in, slots_in, sems):
    width = cot.shape[1]
    coming = copies([(weight, w_in), (ids, ids_in), (slots, slots_in), (cot, out.at[:, pl.ds(0, width)])], sems)
    out[48:, width:] = jnp.zeros((out.shape[0] - 48, META), jnp.bfloat16)
    for copy in coming[:3]:
        copy.wait()
    w = w_in[...]
    hi = w.astype(jnp.bfloat16)
    rest = w - hi.astype(jnp.float32)
    mid = rest.astype(jnp.bfloat16)
    low = (rest - mid.astype(jnp.float32)).astype(jnp.bfloat16)
    rows = [
        ids_in[...].astype(jnp.float32),
        slots_in[...].astype(jnp.float32),
        hi.astype(jnp.float32),
        mid.astype(jnp.float32),
        low.astype(jnp.float32),
        jnp.zeros(low.shape, jnp.float32),
    ]
    out[0:48, width:] = jnp.concatenate(rows, axis=0).astype(jnp.bfloat16)
    coming[3].wait()


def pack(cot, weight, ids, slots):
    return pl.pallas_call(
        pack_kernel,
        name="pack",
        out_shape=jax.ShapeDtypeStruct((cot.shape[0], cot.shape[1] + META), jnp.bfloat16),
        in_specs=[HBM] * 4,
        out_specs=VM,
        scratch_shapes=[pltpu.VMEM(a.shape, a.dtype) for a in (weight, ids, slots)]
        + [pltpu.SemaphoreType.DMA((4,))],
        compiler_params=params(12),
        cost_estimate=cost(2),
    )(*(far_memory(a) for a in (cot, weight, ids, slots)))


def gate(values, after):
    return list(lax.optimization_barrier((tuple(values), tuple(after)))[0])


def build_kernel(kind, me, *refs):
    made, sems = refs[-2:]
    count = made.shape[1]
    blocks, outs = refs[:count], refs[count:-2]
    going = []
    for b in range(count):
        block = blocks[b]
        width = block.shape[1] - META
        routes = block[0:48, width:].astype(jnp.float32)
        expert = routes[0:8].astype(jnp.int32)
        slot = routes[8:16].astype(jnp.int32)
        weight = routes[16:24] + routes[24:32] + routes[32:40]
        x, c = expert // (NY * NC), expert % NC
        if kind == SPLIT:
            x = (x - me[0] + NX) % NX
        if kind != WHOLE:
            c = (c + me[2]) % NC
        here = ((expert // NC) % NY == me[1]) & (slot < CAP)
        code = jnp.where(here, (x * NC + c) * CAP + slot, -1)
        row = lax.broadcasted_iota(jnp.int32, (COLS * CAP, code.shape[1]), 0)
        pick = jnp.zeros(row.shape, jnp.float32)
        scale = jnp.zeros(row.shape, jnp.float32)
        for k in range(code.shape[0]):
            match = row == code[k : k + 1]
            pick = jnp.where(match, 1.0, pick)
            scale = jnp.where(match, weight[k : k + 1], scale)
        scale = jnp.sum(scale, axis=1, keepdims=True)
        pick = pick.astype(jnp.bfloat16)
        step = width // 4
        for at in range(0, width, step):
            rows = (scale * dot(pick, block[:, at : at + step], NN)).astype(jnp.bfloat16)
            for d in range(COLS):
                made[d, b, :, at : at + step] = rows[d * CAP : (d + 1) * CAP]
            if kind != SPLIT:
                cut = (slice(None), b, slice(None), pl.ds(at, step))
                going += copies([(made.at[cut], outs[0].at[cut])], sems, len(going))
    if kind == SPLIT:
        going = copies([(made.at[d], outs[d]) for d in range(COLS)], sems)
    for copy in going:
        copy.wait()


def build(n, me, blocks, kind):
    width = blocks[0].shape[1] - META
    shape = (len(blocks), CAP, width)
    outs = [pltpu.HBM(shape, jnp.bfloat16)] * COLS if kind == SPLIT else [pltpu.HBM((COLS,) + shape, jnp.bfloat16)]
    return pl.pallas_call(
        functools.partial(build_kernel, kind),
        name=f"build_{n}",
        out_shape=outs,
        in_specs=[SM] + [VM] * len(blocks),
        out_specs=[HBM] * len(outs),
        scratch_shapes=[pltpu.VMEM((COLS,) + shape, jnp.bfloat16), pltpu.SemaphoreType.DMA((8,))],
        compiler_params=params(8),
        cost_estimate=cost(COST_BUILD),
    )(me, *blocks)


def places(me, chunk):
    kind, offsets = chunk
    order = [(x, c) for x in range(NX) for c in range(NC)]
    if kind == CROSS:
        order = [(x, (me[2] + dc) % NC) for dc in range(NC) for x in range(NX)]
    if kind == SPLIT:
        order = [((me[0] - x + NX) % NX, (me[2] + c) % NC) for x, c in order]
    return [(x * NY + (me[1] + offset + NY) % NY) * NC + c for x, c in order for offset in offsets]


def fetches(chunk, parts, rows):
    kind, offsets = chunk
    if kind == WHOLE:
        return [(parts[0], rows)]
    if kind == CROSS:
        return [
            (parts[0].at[pl.ds(x * NC, 1)], rows.at[pl.ds(x, 1)]) for x in range(NX)
        ] + [(parts[1], rows.at[pl.ds(NX, NX)])]
    return [(parts[d], rows.at[d]) for d in range(COLS)]


def grads_kernel(chunk, first, last, waits, *refs):
    me, refs = refs[0], refs[1 + waits :]
    count = PARTS[chunk[0]]
    parts, (hidden, amap, bmap), refs = refs[:count], refs[count : count + 3], refs[count + 3 :]
    old_a, old_b = (None, None) if first else refs[:2]
    rest = refs if first else refs[2:]
    hid, tok, a_in, b_in, sems = rest[-5:]
    outs = rest[:-5]
    pairs = [(amap, a_in), (bmap, b_in)]
    pairs += [(hidden.at[src], hid.at[pl.ds(i * CAP, CAP)]) for i, src in enumerate(places(me, chunk))]
    small = len(pairs)
    coming = copies(pairs + fetches(chunk, parts, tok), sems)
    for copy in coming[:small]:
        copy.wait()
    rows, width = hid.shape[0], tok.shape[-1]
    z = dot(hid[...], a_in[...], NT).astype(jnp.bfloat16)
    for copy in coming[small:]:
        copy.wait()
    tokens = tok[...].reshape(rows, width)
    rb = (ADAPTER_SCALE * dot(tokens, b_in[...], NT)).astype(jnp.bfloat16)
    outs[0][...] = rb
    grad_b = ADAPTER_SCALE * dot(z, tokens, TN)
    grad_a = dot(rb, hid[...], TN)
    if old_a is not None:
        grad_b = grad_b + old_b[...]
        grad_a = grad_a + old_a[...]
    if not last:
        outs[1][...] = grad_a
        outs[2][...] = grad_b
    else:
        sent = outs[1]
        wide_b = width // GROUPS
        wide_a = hid.shape[1] // GROUPS
        for z_to in range(GROUPS):
            sent[z_to, :, :wide_b] = grad_b[:, z_to * wide_b : (z_to + 1) * wide_b].astype(jnp.bfloat16)
            sent[z_to, :, wide_b : wide_b + wide_a] = grad_a[:, z_to * wide_a : (z_to + 1) * wide_a].astype(
                jnp.bfloat16
            )


def grads(n, me, parts, hidden, amap, bmap, old, chunk, last, after=()):
    pieces = COLS * len(chunk[1])
    rows = pieces * CAP
    rank, width = bmap.shape
    hidden_width = amap.shape[1]
    shapes = [pltpu.VMEM((rows, rank), jnp.bfloat16)]
    if last:
        piece = width // GROUPS + hidden_width // GROUPS
        shapes += [pltpu.HBM((GROUPS, rank, piece), jnp.bfloat16)]
    else:
        shapes += [
            pltpu.VMEM((rank, hidden_width), jnp.float32),
            pltpu.VMEM((rank, width), jnp.float32),
        ]
    loaded = [far_memory(array) for array in (*parts, hidden, amap, bmap)]
    return pl.pallas_call(
        functools.partial(grads_kernel, chunk, not old, last, len(after)),
        name=f"grads_{n}",
        out_shape=shapes,
        in_specs=[SM] + [ANY] * len(after) + [HBM] * len(loaded) + [VM] * len(old),
        out_specs=[VM] * len(shapes),
        scratch_shapes=[
            pltpu.VMEM((rows, hidden_width), jnp.bfloat16),
            pltpu.VMEM((COLS, len(chunk[1]), CAP, width), jnp.bfloat16),
            pltpu.VMEM(amap.shape, jnp.bfloat16),
            pltpu.VMEM(bmap.shape, jnp.bfloat16),
            pltpu.SemaphoreType.DMA((pieces + 2 + COLS,)),
        ],
        compiler_params=params(10),
        cost_estimate=cost(COST_GRADS),
    )(me, *after, *loaded, *old)


def back_kernel(chunks, more, me, *refs):
    counts = [PARTS[chunk[0]] for chunk in chunks]
    weight, refs = refs[:GROUPS], refs[GROUPS:]
    flat, refs = refs[: sum(counts)], refs[sum(counts) :]
    rbs, amap, refs = refs[: len(chunks)], refs[len(chunks)], refs[len(chunks) + 1 + more :]
    out, wide_w, tok, rb, done, sems, sems_out = refs
    pairs = []
    begin = 0
    for n, chunk in enumerate(chunks):
        pieces = len(chunk[1]) * COLS
        rows = tok.at[pl.ds(begin, pieces)]
        at = sum(counts[:n])
        pairs += fetches(chunk, flat[at : at + counts[n]], rows.reshape(COLS, len(chunk[1]), CAP, tok.shape[-1]))
        rb[begin * CAP : (begin + pieces) * CAP] = rbs[n][...]
        begin += pieces
    coming = copies(pairs + [(weight[d], wide_w.at[d]) for d in range(GROUPS)], sems)
    total = dot(rb[...], amap[...], NN)
    for copy in coming[: len(pairs)]:
        copy.wait()
    rows, wide = rb.shape[0], wide_w.shape[-1]
    for d in range(GROUPS):
        coming[len(pairs) + d].wait()
        z = (me[3] - d + GROUPS) % GROUPS
        g = tok[:, :, pl.ds(pl.multiple_of(z * wide, wide), wide)].reshape(rows, wide)
        total = total + dot(g, wide_w[d], NT)
    done[...] = total.astype(jnp.bfloat16).reshape(done.shape)
    where = [src for chunk in chunks for src in places(me, chunk)]
    for copy in copies([(done.at[i], out.at[src]) for i, src in enumerate(where)], sems_out):
        copy.wait()


def back(n, me, weight, amap, work, chunks, old=()):
    flat = [part for parts, rb in work for part in parts]
    rbs = [rb for parts, rb in work]
    hidden_width = amap.shape[1]
    width = flat[0].shape[-1]
    pieces = sum(COLS * len(chunk[1]) for chunk in chunks)
    return pl.pallas_call(
        functools.partial(back_kernel, chunks, len(old)),
        name=f"back_{n}",
        out_shape=pltpu.HBM((NX * NY * NC, CAP, hidden_width), jnp.bfloat16),
        in_specs=[SM] + [HBM] * (GROUPS + len(flat)) + [VM] * (len(rbs) + 1) + [HBM] * len(old),
        out_specs=HBM,
        input_output_aliases={2 + GROUPS + len(flat) + len(rbs): 0} if old else {},
        scratch_shapes=[
            pltpu.VMEM((GROUPS,) + weight[0].shape, jnp.bfloat16),
            pltpu.VMEM((pieces, CAP, width), jnp.bfloat16),
            pltpu.VMEM((pieces * CAP, amap.shape[0]), jnp.bfloat16),
            pltpu.VMEM((pieces, CAP, hidden_width), jnp.bfloat16),
            pltpu.SemaphoreType.DMA((GROUPS + 2 * COLS * len(work),)),
            pltpu.SemaphoreType.DMA((pieces,)),
        ],
        compiler_params=params(26),
        cost_estimate=cost(COST_BACK),
    )(me, *(far_memory(array) for array in (*weight, *flat)), *rbs, amap, *old)


def spread_kernel(got, out):
    total = jnp.sum(got[...].astype(jnp.float32), axis=0).astype(jnp.bfloat16)
    for d in range(COLS):
        out[d] = total


def spread(got):
    return pl.pallas_call(
        spread_kernel,
        name="spread",
        out_shape=jax.ShapeDtypeStruct((COLS,) + got.shape[1:], got.dtype),
        in_specs=[VM],
        out_specs=VM,
    )(got)


def turn_kernel(where, got, out):
    for y_to in range(NY):
        out[y_to] = got[where[y_to]]


def turn(where, got):
    return pl.pallas_call(
        turn_kernel,
        name="turn",
        out_shape=jax.ShapeDtypeStruct((NY,) + got.shape[1:], got.dtype),
        in_specs=[SM, VM],
        out_specs=VM,
    )(where, got)


def take_kernel(wide_b, where, got, out_a, out_b):
    row = got[where[NY]]
    out_b[...] = row[:, :wide_b]
    out_a[...] = row[:, wide_b:]


def take(where, got, wide_a, wide_b):
    rank = got.shape[1]
    return pl.pallas_call(
        functools.partial(take_kernel, wide_b),
        name="take",
        out_shape=[
            jax.ShapeDtypeStruct((rank, wide_a), got.dtype),
            jax.ShapeDtypeStruct((rank, wide_b), got.dtype),
        ],
        in_specs=[SM, VM],
        out_specs=[VM, VM],
    )(where, got)


def per_device(
    cotangent,
    route_weight,
    expert_ids,
    slot_ids,
    hidden_saved,
    down_weight,
    adapter_a,
    adapter_out_maps,
    rollout_owner,
):
    width = cotangent.shape[1]
    hidden_width = adapter_a.shape[2]
    x = lax.axis_index("x").astype(jnp.int32)
    y = lax.axis_index("y").astype(jnp.int32)
    c = lax.axis_index("core").astype(jnp.int32)
    me = jnp.stack([x, y, c, lax.axis_index("dp").astype(jnp.int32)])
    up = [(i, (i + 1) % NY) for i in range(NY)]
    down = [(i, (i - 1) % NY) for i in range(NY)]
    row = ("x", "core")
    experts = jnp.arange(NX * NY * NC, dtype=jnp.int32)
    takers = (x * NY + jnp.append(jnp.arange(NY, dtype=jnp.int32), y)) * NC + c
    taken = jnp.sum(jnp.where(rollout_owner[None, :] == takers[:, None], experts[None, :], 0), axis=1)
    beside = taken // (NY * NC) * NC + taken % NC
    where = jnp.where(jnp.arange(NY + 1) < NY, beside, taken // NC % NY)

    def steps(dx, dc):
        return [(i * NC + j, (i + dx) % NX * NC + (j + dc) % NC) for i in range(NX) for j in range(NC)]

    def send(built, kind):
        if kind == WHOLE:
            return [lax.all_to_all(built[0], row, 0, 0, tiled=True)]
        if kind == CROSS:
            return [lax.all_to_all(built[0], "x", 0, 0, tiled=True)]
        return [built[0]] + [lax.ppermute(built[d], row, steps(d // NC, d % NC)) for d in range(1, COLS)]

    def cross(parts):
        return parts + [lax.ppermute(parts[0][1::NC], "core", [(0, 1), (1, 0)])]

    own = pack(cotangent, route_weight.T, expert_ids.T, slot_ids.T)
    weight = [down_weight[0]] + [None] * (GROUPS - 1)
    rise = [(i, (i + 1) % GROUPS) for i in range(GROUPS)]
    fall = [(i, (i - 1) % GROUPS) for i in range(GROUPS)]
    hidden = hidden_saved.reshape(NX * NY * NC, CAP, hidden_width)
    amap = adapter_a[0]
    bmap = adapter_out_maps[0]

    kinds = [WHOLE, CROSS, CROSS, WHOLE, SPLIT]
    offsets = [(0,)] + [(-d, d) for d in range(1, NY // 2)] + [(NY // 2,)]
    last = len(offsets) - 1
    chunks = []
    old = ()
    work = []
    whole = []

    def settle(n, after=()):
        nonlocal old
        chunks.append((kinds[n], offsets[n]))
        rb, *old = grads(n, me, whole[n], hidden, amap, bmap, old, chunks[-1], len(chunks) == last + 1, after)
        work.append((whole[n], rb))
        return rb

    either = [(i * NC, (i + 1) % NY * NC) for i in range(NY)] + [(i * NC + 1, (i - 1) % NY * NC + 1) for i in range(NY)]
    held = [own]
    pending = []
    for w in range(1, last + 1):
        low, high = held[0], held[-1]
        if w < last:
            ahead = [lax.ppermute(low, "y", up), lax.ppermute(high, "y", down)]
        else:
            ahead = [lax.ppermute(jnp.where(c == 0, low, high), ("y", "core"), either)]
        done = []
        if w >= 3:
            whole[w - 3] = gate(whole[w - 3], whole[w - 2][:1])
            done.append(settle(w - 3))
        kind = kinds[w - 1]
        built = build(w - 1, me, held, kind)
        parts = send(built, kind)
        whole.append(cross(parts) if kind == CROSS else parts)
        done += pending
        pending = []
        if w != 2:
            step = max(1, w - 1)
            after = built if w == 1 else whole[w - 2]
            rising, falling = gate([weight[step - 1], weight[(1 - step) % GROUPS]], after[:1])
            weight[step] = lax.ppermute(rising, "dp", rise)
            weight[-step] = lax.ppermute(falling, "dp", fall)
            if w < last:
                pending = [weight[step], weight[-step]]
        held = [gate([block], done + [built[0], where])[0] for block in ahead]
    weight[last] = lax.ppermute(weight[last - 1], "dp", rise)
    built = build(last, me, held, kinds[last])
    whole.append(send(built, kinds[last]))
    whole[2] = gate(whole[2], [built[0]])
    settle(2)
    rb = settle(4)
    whole[3] = gate(whole[3], [rb])
    settle(3)

    def turn_back(n, begin, end, filled):
        return back(n, me, weight, amap, work[begin:end], chunks[begin:end], filled)

    got = lax.all_to_all(old[0], "dp", 0, 0, tiled=True)
    filled = turn_back(0, 0, 2, [])
    got, filled = gate([got, filled], [])
    row_items = lax.all_to_all(spread(got), row, 0, 0, tiled=True)
    filled = turn_back(1, 2, 3, [filled])
    row_items, filled = gate([row_items, filled], [])
    column_items = lax.all_to_all(turn(where, row_items), "y", 0, 0, tiled=True)
    grad_hidden = turn_back(2, 3, 5, [filled])
    column_items, grad_hidden = gate([column_items, grad_hidden], [])
    out_a, out_b = take(where, column_items, hidden_width // GROUPS, width // GROUPS)
    return (
        grad_hidden.reshape(1, 1, NX * NY * NC * CAP, hidden_width),
        out_a[None],
        out_b[None],
    )


def solution(mesh):
    parts = Mesh(mesh.devices.reshape(GROUPS, NX, NY, NC), ("dp", "x", "y", "core"))
    every = ("dp", "x", "y", "core")
    expert = ("x", "y", "core")
    return jax.shard_map(
        per_device,
        mesh=parts,
        in_specs=(
            P(every, None),
            P(every, None),
            P(every, None),
            P(every, None),
            P("dp", expert, None, None),
            P(expert, None, "dp"),
            P(expert, None, None),
            P(expert, None, None),
            P(),
        ),
        out_specs=(P("dp", expert, None, None), P(expert, None, "dp"), P(expert, None, "dp")),
        check_vma=False,
    )
```

```python
import functools

import jax
import jax.numpy as jnp
from jax import lax
from jax.experimental import pallas as pl
from jax.experimental.pallas import tpu as pltpu
from jax.sharding import Mesh, PartitionSpec as P

ADAPTER_SCALE = 2.0
COST_BUILD, COST_GRADS, COST_BACK = 16, 3, 10
GROUPS, NX, NY, NC = 8, 4, 8, 2
COLS = NX * NC
CAP = 16
META = 128
MIB = 1024 * 1024
VM = pl.BlockSpec(memory_space=pltpu.VMEM)
HBM = pl.BlockSpec(memory_space=pltpu.HBM)
SM = pl.BlockSpec(memory_space=pltpu.SMEM)
NT = (((1,), (1,)), ((), ()))
TN = (((0,), (0,)), ((), ()))
NN = (((1,), (0,)), ((), ()))


def dot(a, b, dims):
    return lax.dot_general(a, b, dims, preferred_element_type=jnp.float32)


def params(mib):
    return pltpu.CompilerParams(vmem_limit_bytes=mib * MIB)


def cost(us):
    return pl.CostEstimate(flops=int(us * 1.0e9), bytes_accessed=int(us * 3.0e6), transcendentals=0)


def far_memory(array):
    return pltpu.with_memory_space_constraint(array, pltpu.HBM)


def copies(pairs, sems, first=0):
    started = [pltpu.make_async_copy(src, dst, sems.at[first + i]) for i, (src, dst) in enumerate(pairs)]
    for copy in started:
        copy.start()
    return started


def pack_kernel(cot, weight, ids, slots, out, w_in, ids_in, slots_in, sems):
    width = cot.shape[1]
    coming = copies([(weight, w_in), (ids, ids_in), (slots, slots_in), (cot, out.at[:, pl.ds(0, width)])], sems)
    out[48:, width:] = jnp.zeros((out.shape[0] - 48, META), jnp.bfloat16)
    for copy in coming[:3]:
        copy.wait()
    w = w_in[...]
    hi = w.astype(jnp.bfloat16)
    rest = w - hi.astype(jnp.float32)
    mid = rest.astype(jnp.bfloat16)
    low = (rest - mid.astype(jnp.float32)).astype(jnp.bfloat16)
    rows = [
        ids_in[...].astype(jnp.float32),
        slots_in[...].astype(jnp.float32),
        hi.astype(jnp.float32),
        mid.astype(jnp.float32),
        low.astype(jnp.float32),
        jnp.zeros(low.shape, jnp.float32),
    ]
    out[0:48, width:] = jnp.concatenate(rows, axis=0).astype(jnp.bfloat16)
    coming[3].wait()


def pack(cot, weight, ids, slots):
    return pl.pallas_call(
        pack_kernel,
        name="pack",
        out_shape=jax.ShapeDtypeStruct((cot.shape[0], cot.shape[1] + META), jnp.bfloat16),
        in_specs=[HBM] * 4,
        out_specs=VM,
        scratch_shapes=[pltpu.VMEM(a.shape, a.dtype) for a in (weight, ids, slots)]
        + [pltpu.SemaphoreType.DMA((4,))],
        compiler_params=params(12),
        cost_estimate=cost(2),
    )(*(far_memory(a) for a in (cot, weight, ids, slots)))


def gate(values, after):
    return list(lax.optimization_barrier((tuple(values), tuple(after)))[0])


def build_kernel(me, *refs):
    blocks, (out, made, sems) = refs[:-3], refs[-3:]
    count = made.shape[1]
    going = []
    for b in range(count):
        block = blocks[b]
        width = block.shape[1] - META
        routes = block[0:48, width:].astype(jnp.float32)
        expert = routes[0:8].astype(jnp.int32)
        slot = routes[8:16].astype(jnp.int32)
        weight = routes[16:24] + routes[24:32] + routes[32:40]
        x, c = expert // (NY * NC), expert % NC
        here = ((expert // NC) % NY == me[1]) & (slot < CAP)
        code = jnp.where(here, (x * NC + c) * CAP + slot, -1)
        row = lax.broadcasted_iota(jnp.int32, (COLS * CAP, code.shape[1]), 0)
        pick = jnp.zeros(row.shape, jnp.float32)
        scale = jnp.zeros(row.shape, jnp.float32)
        for k in range(code.shape[0]):
            match = row == code[k : k + 1]
            pick = jnp.where(match, 1.0, pick)
            scale = jnp.where(match, weight[k : k + 1], scale)
        scale = jnp.sum(scale, axis=1, keepdims=True)
        pick = pick.astype(jnp.bfloat16)
        step = width // 4
        for at in range(0, width, step):
            rows = (scale * dot(pick, block[:, at : at + step], NN)).astype(jnp.bfloat16)
            for d in range(COLS):
                made[d, b, :, at : at + step] = rows[d * CAP : (d + 1) * CAP]
            cut = (slice(None), b, slice(None), pl.ds(at, step))
            going += copies([(made.at[cut], out.at[cut])], sems, len(going))
    for copy in going:
        copy.wait()


def build(n, me, blocks):
    width = blocks[0].shape[1] - META
    shape = (len(blocks), CAP, width)
    return pl.pallas_call(
        build_kernel,
        name=f"build_{n}",
        out_shape=pltpu.HBM((COLS,) + shape, jnp.bfloat16),
        in_specs=[SM] + [VM] * len(blocks),
        out_specs=HBM,
        scratch_shapes=[pltpu.VMEM((COLS,) + shape, jnp.bfloat16), pltpu.SemaphoreType.DMA((8,))],
        compiler_params=params(8),
        cost_estimate=cost(COST_BUILD),
    )(me, *blocks)


def places(me, offsets):
    order = [(x, c) for x in range(NX) for c in range(NC)]
    return [(x * NY + (me[1] + offset + NY) % NY) * NC + c for x, c in order for offset in offsets]


def grads_kernel(chunk, first, last, me, part, hidden, amap, bmap, *refs):
    old_a, old_b = (None, None) if first else refs[:2]
    rest = refs if first else refs[2:]
    hid, tok, a_in, b_in, sems = rest[-5:]
    outs = rest[:-5]
    pairs = [(amap, a_in), (bmap, b_in)]
    pairs += [(hidden.at[src], hid.at[pl.ds(i * CAP, CAP)]) for i, src in enumerate(places(me, chunk))]
    small = len(pairs)
    coming = copies(pairs + [(part, tok)], sems)
    for copy in coming[:small]:
        copy.wait()
    rows, width = hid.shape[0], tok.shape[-1]
    z = dot(hid[...], a_in[...], NT).astype(jnp.bfloat16)
    for copy in coming[small:]:
        copy.wait()
    tokens = tok[...].reshape(rows, width)
    rb = (ADAPTER_SCALE * dot(tokens, b_in[...], NT)).astype(jnp.bfloat16)
    outs[0][...] = rb
    grad_b = ADAPTER_SCALE * dot(z, tokens, TN)
    grad_a = dot(rb, hid[...], TN)
    if old_a is not None:
        grad_b = grad_b + old_b[...]
        grad_a = grad_a + old_a[...]
    if not last:
        outs[1][...] = grad_a
        outs[2][...] = grad_b
    else:
        sent = outs[1]
        wide_b = width // GROUPS
        wide_a = hid.shape[1] // GROUPS
        for z_to in range(GROUPS):
            sent[z_to, :, :wide_b] = grad_b[:, z_to * wide_b : (z_to + 1) * wide_b].astype(jnp.bfloat16)
            sent[z_to, :, wide_b : wide_b + wide_a] = grad_a[:, z_to * wide_a : (z_to + 1) * wide_a].astype(
                jnp.bfloat16
            )


def grads(n, me, part, hidden, amap, bmap, old, chunk, last):
    pieces = COLS * len(chunk)
    rows = pieces * CAP
    rank, width = bmap.shape
    hidden_width = amap.shape[1]
    shapes = [pltpu.VMEM((rows, rank), jnp.bfloat16)]
    if last:
        piece = width // GROUPS + hidden_width // GROUPS
        shapes += [pltpu.HBM((GROUPS, rank, piece), jnp.bfloat16)]
    else:
        shapes += [
            pltpu.VMEM((rank, hidden_width), jnp.float32),
            pltpu.VMEM((rank, width), jnp.float32),
        ]
    loaded = [far_memory(array) for array in (part, hidden, amap, bmap)]
    return pl.pallas_call(
        functools.partial(grads_kernel, chunk, not old, last),
        name=f"grads_{n}",
        out_shape=shapes,
        in_specs=[SM] + [HBM] * len(loaded) + [VM] * len(old),
        out_specs=[VM] * len(shapes),
        scratch_shapes=[
            pltpu.VMEM((rows, hidden_width), jnp.bfloat16),
            pltpu.VMEM(part.shape, jnp.bfloat16),
            pltpu.VMEM(amap.shape, jnp.bfloat16),
            pltpu.VMEM(bmap.shape, jnp.bfloat16),
            pltpu.SemaphoreType.DMA((pieces + 3,)),
        ],
        compiler_params=params(10),
        cost_estimate=cost(COST_GRADS),
    )(me, *loaded, *old)


def back_kernel(chunks, more, me, *refs):
    count = len(chunks)
    weight, parts, refs = refs[:GROUPS], refs[GROUPS : GROUPS + count], refs[GROUPS + count :]
    rbs, amap, refs = refs[:count], refs[count], refs[count + 1 + more :]
    out, wide_w, tok, rb, done, sems, sems_out = refs
    pairs = []
    begin = 0
    for part, own_rb in zip(parts, rbs):
        pieces = own_rb.shape[0] // CAP
        pairs.append((part, tok.at[pl.ds(begin, pieces)].reshape(*part.shape)))
        rb[begin * CAP : (begin + pieces) * CAP] = own_rb[...]
        begin += pieces
    coming = copies(pairs + [(weight[d], wide_w.at[d]) for d in range(GROUPS)], sems)
    total = dot(rb[...], amap[...], NN)
    for copy in coming[: len(pairs)]:
        copy.wait()
    rows, wide = rb.shape[0], wide_w.shape[-1]
    for d in range(GROUPS):
        coming[len(pairs) + d].wait()
        z = (me[3] - d + GROUPS) % GROUPS
        g = tok[:, :, pl.ds(pl.multiple_of(z * wide, wide), wide)].reshape(rows, wide)
        total = total + dot(g, wide_w[d], NT)
    done[...] = total.astype(jnp.bfloat16).reshape(done.shape)
    where = [src for chunk in chunks for src in places(me, chunk)]
    for copy in copies([(done.at[i], out.at[src]) for i, src in enumerate(where)], sems_out):
        copy.wait()


def back(n, me, weight, amap, work, chunks, old=()):
    parts = [part for part, rb in work]
    rbs = [rb for parts, rb in work]
    hidden_width = amap.shape[1]
    width = parts[0].shape[-1]
    pieces = sum(COLS * len(chunk) for chunk in chunks)
    return pl.pallas_call(
        functools.partial(back_kernel, chunks, len(old)),
        name=f"back_{n}",
        out_shape=pltpu.HBM((NX * NY * NC, CAP, hidden_width), jnp.bfloat16),
        in_specs=[SM] + [HBM] * (GROUPS + len(parts)) + [VM] * (len(rbs) + 1) + [HBM] * len(old),
        out_specs=HBM,
        input_output_aliases={2 + GROUPS + len(parts) + len(rbs): 0} if old else {},
        scratch_shapes=[
            pltpu.VMEM((GROUPS,) + weight[0].shape, jnp.bfloat16),
            pltpu.VMEM((pieces, CAP, width), jnp.bfloat16),
            pltpu.VMEM((pieces * CAP, amap.shape[0]), jnp.bfloat16),
            pltpu.VMEM((pieces, CAP, hidden_width), jnp.bfloat16),
            pltpu.SemaphoreType.DMA((GROUPS + len(parts),)),
            pltpu.SemaphoreType.DMA((pieces,)),
        ],
        compiler_params=params(26),
        cost_estimate=cost(COST_BACK),
    )(me, *(far_memory(array) for array in (*weight, *parts)), *rbs, amap, *old)


def spread_kernel(got, out):
    total = jnp.sum(got[...].astype(jnp.float32), axis=0).astype(jnp.bfloat16)
    for d in range(COLS):
        out[d] = total


def spread(got):
    return pl.pallas_call(
        spread_kernel,
        name="spread",
        out_shape=jax.ShapeDtypeStruct((COLS,) + got.shape[1:], got.dtype),
        in_specs=[VM],
        out_specs=VM,
    )(got)


def turn_kernel(where, got, out):
    for y_to in range(NY):
        out[y_to] = got[where[y_to]]


def turn(where, got):
    return pl.pallas_call(
        turn_kernel,
        name="turn",
        out_shape=jax.ShapeDtypeStruct((NY,) + got.shape[1:], got.dtype),
        in_specs=[SM, VM],
        out_specs=VM,
    )(where, got)


def take_kernel(wide_b, where, got, out_a, out_b):
    row = got[where[NY]]
    out_b[...] = row[:, :wide_b]
    out_a[...] = row[:, wide_b:]


def take(where, got, wide_a, wide_b):
    rank = got.shape[1]
    return pl.pallas_call(
        functools.partial(take_kernel, wide_b),
        name="take",
        out_shape=[
            jax.ShapeDtypeStruct((rank, wide_a), got.dtype),
            jax.ShapeDtypeStruct((rank, wide_b), got.dtype),
        ],
        in_specs=[SM, VM],
        out_specs=[VM, VM],
    )(where, got)


def per_device(
    cotangent,
    route_weight,
    expert_ids,
    slot_ids,
    hidden_saved,
    down_weight,
    adapter_a,
    adapter_out_maps,
    rollout_owner,
):
    width = cotangent.shape[1]
    hidden_width = adapter_a.shape[2]
    x = lax.axis_index("x").astype(jnp.int32)
    y = lax.axis_index("y").astype(jnp.int32)
    c = lax.axis_index("core").astype(jnp.int32)
    me = jnp.stack([x, y, c, lax.axis_index("dp").astype(jnp.int32)])
    up = [(i, (i + 1) % NY) for i in range(NY)]
    down = [(i, (i - 1) % NY) for i in range(NY)]
    row = ("x", "core")
    experts = jnp.arange(NX * NY * NC, dtype=jnp.int32)
    takers = (x * NY + jnp.append(jnp.arange(NY, dtype=jnp.int32), y)) * NC + c
    taken = jnp.sum(jnp.where(rollout_owner[None, :] == takers[:, None], experts[None, :], 0), axis=1)
    beside = taken // (NY * NC) * NC + taken % NC
    where = jnp.where(jnp.arange(NY + 1) < NY, beside, taken // NC % NY)

    def send(built):
        return lax.all_to_all(built, row, 0, 0, tiled=True)

    own = pack(cotangent, route_weight.T, expert_ids.T, slot_ids.T)
    weight = [down_weight[0]] + [None] * (GROUPS - 1)
    rise = [(i, (i + 1) % GROUPS) for i in range(GROUPS)]
    fall = [(i, (i - 1) % GROUPS) for i in range(GROUPS)]
    hidden = hidden_saved.reshape(NX * NY * NC, CAP, hidden_width)
    amap = adapter_a[0]
    bmap = adapter_out_maps[0]

    chunks = [(0,)] + [(-d, d) for d in range(1, NY // 2)] + [(NY // 2,)]
    last = len(chunks) - 1
    old = ()
    work = []
    sent = []

    def settle(n):
        nonlocal old
        rb, *old = grads(n, me, sent[n], hidden, amap, bmap, old, chunks[n], n == last)
        work.append((sent[n], rb))
        return rb

    either = [(i * NC, (i + 1) % NY * NC) for i in range(NY)] + [(i * NC + 1, (i - 1) % NY * NC + 1) for i in range(NY)]
    held = [own]
    pending = []
    for w in range(1, last + 1):
        low, high = held[0], held[-1]
        if w < last:
            ahead = [lax.ppermute(low, "y", up), lax.ppermute(high, "y", down)]
        else:
            ahead = [lax.ppermute(jnp.where(c == 0, low, high), ("y", "core"), either)]
        done = []
        if w >= 3:
            sent[w - 3] = gate([sent[w - 3]], [sent[w - 2]])[0]
            done.append(settle(w - 3))
        built = build(w - 1, me, held)
        sent.append(send(built))
        done += pending
        pending = []
        if w != 2:
            step = max(1, w - 1)
            after = built if w == 1 else sent[w - 2]
            rising, falling = gate([weight[step - 1], weight[(1 - step) % GROUPS]], [after])
            weight[step] = lax.ppermute(rising, "dp", rise)
            weight[-step] = lax.ppermute(falling, "dp", fall)
            if w < last:
                pending = [weight[step], weight[-step]]
        held = [gate([block], done + [built, where])[0] for block in ahead]
    weight[last] = lax.ppermute(weight[last - 1], "dp", rise)
    rb = settle(2)
    built = build(last, me, gate(held, [rb]))
    sent.append(send(built))
    sent[3] = gate([sent[3]], [weight[-3]])[0]
    rb = settle(3)
    sent[4] = gate([sent[4]], [rb])[0]
    settle(4)

    def turn_back(n, begin, end, filled):
        return back(n, me, weight, amap, work[begin:end], chunks[begin:end], filled)

    got = lax.all_to_all(old[0], "dp", 0, 0, tiled=True)
    filled = turn_back(0, 0, 2, [])
    got, filled = gate([got, filled], [])
    row_items = lax.all_to_all(spread(got), row, 0, 0, tiled=True)
    filled = turn_back(1, 2, 3, [filled])
    row_items, filled = gate([row_items, filled], [])
    column_items = lax.all_to_all(turn(where, row_items), "y", 0, 0, tiled=True)
    grad_hidden = turn_back(2, 3, 5, [filled])
    column_items, grad_hidden = gate([column_items, grad_hidden], [])
    out_a, out_b = take(where, column_items, hidden_width // GROUPS, width // GROUPS)
    return (
        grad_hidden.reshape(1, 1, NX * NY * NC * CAP, hidden_width),
        out_a[None],
        out_b[None],
    )


def solution(mesh):
    parts = Mesh(mesh.devices.reshape(GROUPS, NX, NY, NC), ("dp", "x", "y", "core"))
    every = ("dp", "x", "y", "core")
    expert = ("x", "y", "core")
    return jax.shard_map(
        per_device,
        mesh=parts,
        in_specs=(
            P(every, None),
            P(every, None),
            P(every, None),
            P(every, None),
            P("dp", expert, None, None),
            P(expert, None, "dp"),
            P(expert, None, None),
            P(expert, None, None),
            P(),
        ),
        out_specs=(P("dp", expert, None, None), P(expert, None, "dp"), P(expert, None, "dp")),
        check_vma=False,
    )
```

```python
import functools

import jax
import jax.numpy as jnp
from jax import lax
from jax.experimental import pallas as pl
from jax.experimental.pallas import tpu as pltpu
from jax.sharding import Mesh, PartitionSpec as P

ADAPTER_SCALE = 2.0
COST_BUILD, COST_GRADS, COST_BACK = 16, 3, 10
GROUPS, NX, NY, NC = 8, 4, 8, 2
COLS = NX * NC
CAP = 16
META = 128
MIB = 1024 * 1024
VM = pl.BlockSpec(memory_space=pltpu.VMEM)
HBM = pl.BlockSpec(memory_space=pltpu.HBM)
SM = pl.BlockSpec(memory_space=pltpu.SMEM)
NT = (((1,), (1,)), ((), ()))
TN = (((0,), (0,)), ((), ()))
NN = (((1,), (0,)), ((), ()))


def dot(a, b, dims):
    return lax.dot_general(a, b, dims, preferred_element_type=jnp.float32)


def params(mib):
    return pltpu.CompilerParams(vmem_limit_bytes=mib * MIB)


def cost(us):
    return pl.CostEstimate(flops=int(us * 1.0e9), bytes_accessed=int(us * 3.0e6), transcendentals=0)


def far_memory(array):
    return pltpu.with_memory_space_constraint(array, pltpu.HBM)


def copies(pairs, sems, first=0):
    started = [pltpu.make_async_copy(src, dst, sems.at[first + i]) for i, (src, dst) in enumerate(pairs)]
    for copy in started:
        copy.start()
    return started


def pack_kernel(cot, weight, ids, slots, out, w_in, ids_in, slots_in, sems):
    width = cot.shape[1]
    coming = copies([(weight, w_in), (ids, ids_in), (slots, slots_in), (cot, out.at[:, pl.ds(0, width)])], sems)
    out[48:, width:] = jnp.zeros((out.shape[0] - 48, META), jnp.bfloat16)
    for copy in coming[:3]:
        copy.wait()
    w = w_in[...]
    hi = w.astype(jnp.bfloat16)
    rest = w - hi.astype(jnp.float32)
    mid = rest.astype(jnp.bfloat16)
    low = (rest - mid.astype(jnp.float32)).astype(jnp.bfloat16)
    rows = [
        ids_in[...].astype(jnp.float32),
        slots_in[...].astype(jnp.float32),
        hi.astype(jnp.float32),
        mid.astype(jnp.float32),
        low.astype(jnp.float32),
        jnp.zeros(low.shape, jnp.float32),
    ]
    out[0:48, width:] = jnp.concatenate(rows, axis=0).astype(jnp.bfloat16)
    coming[3].wait()


def pack(cot, weight, ids, slots):
    return pl.pallas_call(
        pack_kernel,
        name="pack",
        out_shape=jax.ShapeDtypeStruct((cot.shape[0], cot.shape[1] + META), jnp.bfloat16),
        in_specs=[HBM] * 4,
        out_specs=VM,
        scratch_shapes=[pltpu.VMEM(a.shape, a.dtype) for a in (weight, ids, slots)]
        + [pltpu.SemaphoreType.DMA((4,))],
        compiler_params=params(12),
        cost_estimate=cost(2),
    )(*(far_memory(a) for a in (cot, weight, ids, slots)))


def gate(values, after):
    return list(lax.optimization_barrier((tuple(values), tuple(after)))[0])


def build_kernel(me, *refs):
    blocks, (out, made, sems) = refs[:-3], refs[-3:]
    count = made.shape[1]
    going = []
    for b in range(count):
        block = blocks[b]
        width = block.shape[1] - META
        routes = block[0:48, width:].astype(jnp.float32)
        expert = routes[0:8].astype(jnp.int32)
        slot = routes[8:16].astype(jnp.int32)
        weight = routes[16:24] + routes[24:32] + routes[32:40]
        x, c = expert // (NY * NC), expert % NC
        here = ((expert // NC) % NY == me[1]) & (slot < CAP)
        code = jnp.where(here, (x * NC + c) * CAP + slot, -1)
        row = lax.broadcasted_iota(jnp.int32, (COLS * CAP, code.shape[1]), 0)
        pick = jnp.zeros(row.shape, jnp.float32)
        scale = jnp.zeros(row.shape, jnp.float32)
        for k in range(code.shape[0]):
            match = row == code[k : k + 1]
            pick = jnp.where(match, 1.0, pick)
            scale = jnp.where(match, weight[k : k + 1], scale)
        scale = jnp.sum(scale, axis=1, keepdims=True)
        pick = pick.astype(jnp.bfloat16)
        step = width // 4
        for at in range(0, width, step):
            rows = (scale * dot(pick, block[:, at : at + step], NN)).astype(jnp.bfloat16)
            for d in range(COLS):
                made[d, b, :, at : at + step] = rows[d * CAP : (d + 1) * CAP]
            cut = (slice(None), b, slice(None), pl.ds(at, step))
            going += copies([(made.at[cut], out.at[cut])], sems, len(going))
    for copy in going:
        copy.wait()


def build(n, me, blocks):
    width = blocks[0].shape[1] - META
    shape = (len(blocks), CAP, width)
    return pl.pallas_call(
        build_kernel,
        name=f"build_{n}",
        out_shape=pltpu.HBM((COLS,) + shape, jnp.bfloat16),
        in_specs=[SM] + [VM] * len(blocks),
        out_specs=HBM,
        scratch_shapes=[pltpu.VMEM((COLS,) + shape, jnp.bfloat16), pltpu.SemaphoreType.DMA((8,))],
        compiler_params=params(8),
        cost_estimate=cost(COST_BUILD),
    )(me, *blocks)


def places(me, offsets):
    order = [(x, c) for x in range(NX) for c in range(NC)]
    return [(x * NY + (me[1] + offset + NY) % NY) * NC + c for x, c in order for offset in offsets]


def grads_kernel(chunk, first, last, me, part, hidden, amap, bmap, *refs):
    old_a, old_b = (None, None) if first else refs[:2]
    rest = refs if first else refs[2:]
    hid, tok, a_in, b_in, sems = rest[-5:]
    outs = rest[:-5]
    pairs = [(amap, a_in), (bmap, b_in)]
    pairs += [(hidden.at[src], hid.at[pl.ds(i * CAP, CAP)]) for i, src in enumerate(places(me, chunk))]
    small = len(pairs)
    coming = copies(pairs + ([] if last else [(part, tok)]), sems)
    for copy in coming[:small]:
        copy.wait()
    rows, width = hid.shape[0], tok.shape[-1]
    z = dot(hid[...], a_in[...], NT).astype(jnp.bfloat16)
    for copy in coming[small:]:
        copy.wait()
    tokens = (part if last else tok)[...].reshape(rows, width)
    rb = (ADAPTER_SCALE * dot(tokens, b_in[...], NT)).astype(jnp.bfloat16)
    outs[0][...] = rb
    grad_b = ADAPTER_SCALE * dot(z, tokens, TN)
    grad_a = dot(rb, hid[...], TN)
    if old_a is not None:
        grad_b = grad_b + old_b[...]
        grad_a = grad_a + old_a[...]
    if not last:
        outs[1][...] = grad_a
        outs[2][...] = grad_b
    else:
        sent = outs[1]
        wide_b = width // GROUPS
        wide_a = hid.shape[1] // GROUPS
        for z_to in range(GROUPS):
            sent[z_to, :, :wide_b] = grad_b[:, z_to * wide_b : (z_to + 1) * wide_b].astype(jnp.bfloat16)
            sent[z_to, :, wide_b : wide_b + wide_a] = grad_a[:, z_to * wide_a : (z_to + 1) * wide_a].astype(
                jnp.bfloat16
            )


def grads(n, me, part, hidden, amap, bmap, old, chunk, last):
    pieces = COLS * len(chunk)
    rows = pieces * CAP
    rank, width = bmap.shape
    hidden_width = amap.shape[1]
    shapes = [pltpu.VMEM((rows, rank), jnp.bfloat16)]
    if last:
        piece = width // GROUPS + hidden_width // GROUPS
        shapes += [pltpu.HBM((GROUPS, rank, piece), jnp.bfloat16)]
    else:
        shapes += [
            pltpu.VMEM((rank, hidden_width), jnp.float32),
            pltpu.VMEM((rank, width), jnp.float32),
        ]
    loaded = [part if last else far_memory(part)] + [far_memory(array) for array in (hidden, amap, bmap)]
    return pl.pallas_call(
        functools.partial(grads_kernel, chunk, not old, last),
        name=f"grads_{n}",
        out_shape=shapes,
        in_specs=[SM] + [VM if last else HBM] + [HBM] * 3 + [VM] * len(old),
        out_specs=[VM] * len(shapes),
        scratch_shapes=[
            pltpu.VMEM((rows, hidden_width), jnp.bfloat16),
            pltpu.VMEM(part.shape, jnp.bfloat16),
            pltpu.VMEM(amap.shape, jnp.bfloat16),
            pltpu.VMEM(bmap.shape, jnp.bfloat16),
            pltpu.SemaphoreType.DMA((pieces + 3,)),
        ],
        compiler_params=params(10),
        cost_estimate=cost(COST_GRADS),
    )(me, *loaded, *old)


def back_kernel(chunks, more, me, *refs):
    count = len(chunks)
    weight, parts, refs = refs[:GROUPS], refs[GROUPS : GROUPS + count], refs[GROUPS + count :]
    rbs, amap, refs = refs[:count], refs[count], refs[count + 1 + more :]
    out, wide_w, tok, rb, done, sems, sems_out = refs
    pairs = []
    begin = 0
    for part, own_rb in zip(parts, rbs):
        pieces = own_rb.shape[0] // CAP
        pairs.append((part, tok.at[pl.ds(begin, pieces)].reshape(*part.shape)))
        rb[begin * CAP : (begin + pieces) * CAP] = own_rb[...]
        begin += pieces
    coming = copies(pairs + [(weight[d], wide_w.at[d]) for d in range(GROUPS)], sems)
    total = dot(rb[...], amap[...], NN)
    for copy in coming[: len(pairs)]:
        copy.wait()
    rows, wide = rb.shape[0], wide_w.shape[-1]
    for d in range(GROUPS):
        coming[len(pairs) + d].wait()
        z = (me[3] - d + GROUPS) % GROUPS
        g = tok[:, :, pl.ds(pl.multiple_of(z * wide, wide), wide)].reshape(rows, wide)
        total = total + dot(g, wide_w[d], NT)
    done[...] = total.astype(jnp.bfloat16).reshape(done.shape)
    where = [src for chunk in chunks for src in places(me, chunk)]
    for copy in copies([(done.at[i], out.at[src]) for i, src in enumerate(where)], sems_out):
        copy.wait()


def back(n, me, weight, amap, work, chunks, old=()):
    parts = [part for part, rb in work]
    rbs = [rb for parts, rb in work]
    hidden_width = amap.shape[1]
    width = parts[0].shape[-1]
    pieces = sum(COLS * len(chunk) for chunk in chunks)
    return pl.pallas_call(
        functools.partial(back_kernel, chunks, len(old)),
        name=f"back_{n}",
        out_shape=pltpu.HBM((NX * NY * NC, CAP, hidden_width), jnp.bfloat16),
        in_specs=[SM] + [HBM] * (GROUPS + len(parts)) + [VM] * (len(rbs) + 1) + [HBM] * len(old),
        out_specs=HBM,
        input_output_aliases={2 + GROUPS + len(parts) + len(rbs): 0} if old else {},
        scratch_shapes=[
            pltpu.VMEM((GROUPS,) + weight[0].shape, jnp.bfloat16),
            pltpu.VMEM((pieces, CAP, width), jnp.bfloat16),
            pltpu.VMEM((pieces * CAP, amap.shape[0]), jnp.bfloat16),
            pltpu.VMEM((pieces, CAP, hidden_width), jnp.bfloat16),
            pltpu.SemaphoreType.DMA((GROUPS + len(parts),)),
            pltpu.SemaphoreType.DMA((pieces,)),
        ],
        compiler_params=params(26),
        cost_estimate=cost(COST_BACK),
    )(me, *(far_memory(array) for array in (*weight, *parts)), *rbs, amap, *old)


def spread_kernel(got, out):
    total = jnp.sum(got[...].astype(jnp.float32), axis=0).astype(jnp.bfloat16)
    for d in range(COLS):
        out[d] = total


def spread(got):
    return pl.pallas_call(
        spread_kernel,
        name="spread",
        out_shape=jax.ShapeDtypeStruct((COLS,) + got.shape[1:], got.dtype),
        in_specs=[VM],
        out_specs=VM,
    )(got)


def turn_kernel(where, got, out):
    for y_to in range(NY):
        out[y_to] = got[where[y_to]]


def turn(where, got):
    return pl.pallas_call(
        turn_kernel,
        name="turn",
        out_shape=jax.ShapeDtypeStruct((NY,) + got.shape[1:], got.dtype),
        in_specs=[SM, VM],
        out_specs=VM,
    )(where, got)


def take_kernel(wide_b, where, got, out_a, out_b):
    row = got[where[NY]]
    out_b[...] = row[:, :wide_b]
    out_a[...] = row[:, wide_b:]


def take(where, got, wide_a, wide_b):
    rank = got.shape[1]
    return pl.pallas_call(
        functools.partial(take_kernel, wide_b),
        name="take",
        out_shape=[
            jax.ShapeDtypeStruct((rank, wide_a), got.dtype),
            jax.ShapeDtypeStruct((rank, wide_b), got.dtype),
        ],
        in_specs=[SM, VM],
        out_specs=[VM, VM],
    )(where, got)


def per_device(
    cotangent,
    route_weight,
    expert_ids,
    slot_ids,
    hidden_saved,
    down_weight,
    adapter_a,
    adapter_out_maps,
    rollout_owner,
):
    width = cotangent.shape[1]
    hidden_width = adapter_a.shape[2]
    x = lax.axis_index("x").astype(jnp.int32)
    y = lax.axis_index("y").astype(jnp.int32)
    c = lax.axis_index("core").astype(jnp.int32)
    me = jnp.stack([x, y, c, lax.axis_index("dp").astype(jnp.int32)])
    up = [(i, (i + 1) % NY) for i in range(NY)]
    down = [(i, (i - 1) % NY) for i in range(NY)]
    row = ("x", "core")
    experts = jnp.arange(NX * NY * NC, dtype=jnp.int32)
    takers = (x * NY + jnp.append(jnp.arange(NY, dtype=jnp.int32), y)) * NC + c
    taken = jnp.sum(jnp.where(rollout_owner[None, :] == takers[:, None], experts[None, :], 0), axis=1)
    beside = taken // (NY * NC) * NC + taken % NC
    where = jnp.where(jnp.arange(NY + 1) < NY, beside, taken // NC % NY)

    def send(built):
        return lax.all_to_all(built, row, 0, 0, tiled=True)

    own = pack(cotangent, route_weight.T, expert_ids.T, slot_ids.T)
    weight = [down_weight[0]] + [None] * (GROUPS - 1)
    rise = [(i, (i + 1) % GROUPS) for i in range(GROUPS)]
    fall = [(i, (i - 1) % GROUPS) for i in range(GROUPS)]
    hidden = hidden_saved.reshape(NX * NY * NC, CAP, hidden_width)
    amap = adapter_a[0]
    bmap = adapter_out_maps[0]

    chunks = [(0,)] + [(-d, d) for d in range(1, NY // 2)] + [(NY // 2,)]
    last = len(chunks) - 1
    old = ()
    work = []
    sent = []

    def settle(n):
        nonlocal old
        rb, *old = grads(n, me, sent[n], hidden, amap, bmap, old, chunks[n], n == last)
        work.append((sent[n], rb))
        return rb

    either = [(i * NC, (i + 1) % NY * NC) for i in range(NY)] + [(i * NC + 1, (i - 1) % NY * NC + 1) for i in range(NY)]
    held = [own]
    pending = []
    for w in range(1, last + 1):
        low, high = held[0], held[-1]
        if w < last:
            ahead = [lax.ppermute(low, "y", up), lax.ppermute(high, "y", down)]
        else:
            ahead = [lax.ppermute(jnp.where(c == 0, low, high), ("y", "core"), either)]
        done = []
        if w >= 3:
            sent[w - 3] = gate([sent[w - 3]], [sent[w - 2]])[0]
            done.append(settle(w - 3))
        built = build(w - 1, me, held)
        sent.append(send(built))
        done += pending
        pending = []
        if w != 2:
            step = max(1, w - 1)
            after = built if w == 1 else sent[w - 2]
            rising, falling = gate([weight[step - 1], weight[(1 - step) % GROUPS]], [after])
            weight[step] = lax.ppermute(rising, "dp", rise)
            weight[-step] = lax.ppermute(falling, "dp", fall)
            if w < last:
                pending = [weight[step], weight[-step]]
        held = [gate([block], done + [built, where])[0] for block in ahead]
    weight[last] = lax.ppermute(weight[last - 1], "dp", rise)
    rb = settle(2)
    built = build(last, me, gate(held, [rb]))
    sent.append(send(built))
    sent[3] = gate([sent[3]], [weight[-3]])[0]
    rb = settle(3)
    sent[4] = gate([sent[4]], [rb])[0]
    settle(4)

    def turn_back(n, begin, end, filled):
        return back(n, me, weight, amap, work[begin:end], chunks[begin:end], filled)

    got = lax.all_to_all(old[0], "dp", 0, 0, tiled=True)
    filled = turn_back(0, 0, 2, [])
    got, filled = gate([got, filled], [])
    row_items = lax.all_to_all(spread(got), row, 0, 0, tiled=True)
    filled = turn_back(1, 2, 3, [filled])
    row_items, filled = gate([row_items, filled], [])
    column_items = lax.all_to_all(turn(where, row_items), "y", 0, 0, tiled=True)
    grad_hidden = turn_back(2, 3, 5, [filled])
    column_items, grad_hidden = gate([column_items, grad_hidden], [])
    out_a, out_b = take(where, column_items, hidden_width // GROUPS, width // GROUPS)
    return (
        grad_hidden.reshape(1, 1, NX * NY * NC * CAP, hidden_width),
        out_a[None],
        out_b[None],
    )


def solution(mesh):
    parts = Mesh(mesh.devices.reshape(GROUPS, NX, NY, NC), ("dp", "x", "y", "core"))
    every = ("dp", "x", "y", "core")
    expert = ("x", "y", "core")
    return jax.shard_map(
        per_device,
        mesh=parts,
        in_specs=(
            P(every, None),
            P(every, None),
            P(every, None),
            P(every, None),
            P("dp", expert, None, None),
            P(expert, None, "dp"),
            P(expert, None, None),
            P(expert, None, None),
            P(),
        ),
        out_specs=(P("dp", expert, None, None), P(expert, None, "dp"), P(expert, None, "dp")),
        check_vma=False,
    )
```
